32 devices in a mesh: fsdp: 4 (over y, x), dp: 8 (over z, core).
Axes of the slice: x: 2, y: 2, z: 4, core: 2. Of those that a mesh axis runs over, the one named last changes fastest.
Arguments:
- tokens: bfloat16 [16384, 960], P(('fsdp', 'dp')), may hold values from -6 to 6
- span_table: int32 [8, 8], P('dp'), may hold values from 0 to 7, as said below
- w_query: bfloat16 [960, 960], P('fsdp'), may hold values from -0.1875 to 0.1875
- w_key: bfloat16 [960, 320], P('fsdp'), may hold values from -0.1875 to 0.1875
- w_value: bfloat16 [960, 320], P('fsdp'), may hold values from -0.1875 to 0.1875
- w_out: bfloat16 [960, 960], P('fsdp'), may hold values from -3.5 to 3.5
- w_gate: bfloat16 [960, 2560], P('fsdp'), may hold values from -0.1875 to 0.1875
- w_up: bfloat16 [960, 2560], P('fsdp'), may hold values from -0.1875 to 0.1875
- w_down: bfloat16 [2560, 960], P('fsdp'), may hold values from -0.125 to 0.125
- gain_attn: bfloat16 [960], P('fsdp'), may hold values from 0.099609375 to 1.8984375
- gain_ffn: bfloat16 [960], P('fsdp'), may hold values from 0.099609375 to 1.8984375
- cotangent: bfloat16 [16384, 960], P(('fsdp', 'dp')), may hold values from -6 to 6
Outputs:
- output: bfloat16 [16384, 960], P(('fsdp', 'dp'))
- grad_tokens: float32 [16384, 960], P(('fsdp', 'dp'))
- grad_w_query: float32 [960, 960], P('fsdp')
- grad_w_key: float32 [960, 320], P('fsdp')
- grad_w_value: float32 [960, 320], P('fsdp')
- grad_w_out: float32 [960, 960], P('fsdp')
- grad_w_gate: float32 [960, 2560], P('fsdp')
- grad_w_up: float32 [960, 2560], P('fsdp')
- grad_w_down: float32 [2560, 960], P('fsdp')
- grad_gain_attn: float32 [960], P('fsdp')
- grad_gain_ffn: float32 [960], P('fsdp')
The draws below stay inside these ranges and needn't reach their ends.
Inputs may be any that keep to these rules, and one draw needn't show every extreme that they name: `span_table`: each row is a permutation of the 8 blocks of a sequence over the slots.
All inputs are finite; a program needn't handle non-finite values.
Results may differ from the reference program's by a relative error of at most 0.022.
Values may be sent and summed in bfloat16 or wider, within the bound.
A program may use at most 192 MiB of HBM per device.

```python
import jax
import jax.numpy as jnp
from jax import lax

D = 960
HEADS = 15
KV_HEADS = 5
HEAD_DIM = 64
FF = 2560
TOK_DEV = 512
SEQ_LEN = 2048
KV_WIDTH = 320
SEQS = 1
SPAN = 256
ALL_SEQS = 8
TOKENS = 16384
N_FSDP = 4
N_DP = 8


def draw_span_table(key, part):
    slots = 2 * N_FSDP
    order = jnp.arange(slots, dtype=jnp.int32)
    paired = order // 2
    folded = jnp.where(order % 2 == 0, paired, slots - 1 - paired).astype(jnp.int32)
    flips = jax.random.randint(jax.random.fold_in(key, 11), (ALL_SEQS, 1), 0, 2)
    shifts = jax.random.randint(jax.random.fold_in(key, 12), (ALL_SEQS, 1), 0, N_FSDP)
    base = jnp.where(flips == 1, folded[None, :], order[None, :]).astype(jnp.int32)
    source = ((paired[None, :] + shifts) % N_FSDP * 2 + order[None, :] % 2).astype(jnp.int32)
    return jnp.take_along_axis(base, source, axis=1).astype(jnp.int32)


def shard_levels(stream_key, dims, cuts, low, top_value):
    def one(dim, parts):
        draws = jax.random.uniform(jax.random.fold_in(jax.random.fold_in(stream_key, 6), dim), (parts,), jnp.float32, low / len(cuts), top_value / len(cuts))
        return jnp.repeat(jnp.exp(draws), dims[dim] // parts).reshape((-1,) + (1,) * (len(dims) - dim - 1))

    loudness = one(*cuts[0])
    for cut in cuts[1:]:
        loudness = loudness * one(*cut)
    return loudness


def noise(rng, extent, width, reach, split=(), kind=jnp.bfloat16):
    entries = width * jax.random.normal(rng, extent, jnp.float32)
    if split:
        entries = entries * shard_levels(rng, extent, split, -0.22, 0.18)
    return jnp.clip(entries, -reach, reach).astype(kind)


def setup_inputs(seed: int = 0) -> dict:
    key_of = jax.random.split(jax.random.key(seed), 13)
    return {
        "tokens": noise(key_of[0], (TOKENS, D), 1.0, 6.0, ((0, 32),)),
        "span_table": draw_span_table(jax.random.fold_in(key_of[12], 71), 0),
        "w_query": noise(key_of[2], (D, D), D ** -0.5, 0.1875, ((0, 4),)),
        "w_key": noise(key_of[3], (D, KV_WIDTH), D ** -0.5, 0.1875, ((0, 4),)),
        "w_value": noise(key_of[4], (D, KV_WIDTH), D ** -0.5, 0.1875, ((0, 4),)),
        "w_out": noise(key_of[5], (D, D), (D * 8 // SEQ_LEN) ** -0.5, 3.5, ((0, 4),)),
        "w_gate": noise(key_of[6], (D, FF), D ** -0.5, 0.1875, ((0, 4),)),
        "w_up": noise(key_of[7], (D, FF), D ** -0.5, 0.1875, ((0, 4),)),
        "w_down": noise(key_of[8], (FF, D), FF ** -0.5, 0.125, ((0, 4),)),
        "gain_attn": jnp.clip(1.0 + 0.18 * jax.random.normal(key_of[9], (D,), jnp.float32), 0.099609375, 1.8984375).astype(jnp.bfloat16),
        "gain_ffn": jnp.clip(1.0 + 0.18 * jax.random.normal(key_of[10], (D,), jnp.float32), 0.099609375, 1.8984375).astype(jnp.bfloat16),
        "cotangent": noise(key_of[11], (TOKENS, D), 1.0, 6.0, ((0, 32),)),
    }


@jax.custom_vjp
def low(v):
    return lax.optimization_barrier(v.astype(jnp.bfloat16)).astype(jnp.float32)

@jax.custom_vjp
def low_back(v):
    return v

def low_keep(v):
    return (low(v), None)

def low_pass(kept, grad):
    return (grad,)

def back_keep(v):
    return (v, None)

def back_low(kept, grad):
    return (low(grad),)
low.defvjp(low_keep, low_pass)
low_back.defvjp(back_keep, back_low)
epsilon = 1e-05
rope_base = 100000.0

def matmul(left, right):
    return jnp.dot(left, right, precision=lax.Precision.HIGHEST)

def rope_tables(places):
    half_dim = HEAD_DIM // 2
    rates = rope_base ** (-2.0 * jnp.arange(half_dim, dtype=jnp.float32) / HEAD_DIM)
    angles = places.astype(jnp.float32)[:, None] * rates[None, :]
    return (jnp.cos(angles)[:, None, :], jnp.sin(angles)[:, None, :])

def rotate(field, cosine, sine_part):
    half_dim = field.shape[-1] // 2
    first = field[..., :half_dim]
    second = field[..., half_dim:]
    return jnp.concatenate([first * cosine - second * sine_part, second * cosine + first * sine_part], axis=-1)

def rms_norm(values, gain):
    return values * lax.rsqrt(lax.optimization_barrier(jnp.mean(values * values, axis=-1, keepdims=True)) + epsilon) * gain

def group_places(table_rows):
    slots = table_rows.reshape(SEQS, N_FSDP, 2).transpose(1, 0, 2)
    offsets = jnp.arange(SPAN, dtype=jnp.int32)
    return (slots[..., None] * SPAN + offsets).reshape(-1).astype(jnp.int32)

def by_sequence(field):
    shaped = field.reshape((N_FSDP, SEQS, 2 * SPAN) + field.shape[1:])
    return jnp.swapaxes(shaped, 0, 1).reshape((SEQS, N_FSDP * 2 * SPAN) + field.shape[1:])

def from_sequence(field):
    shaped = field.reshape((SEQS, N_FSDP, 2 * SPAN) + field.shape[2:])
    return jnp.swapaxes(shaped, 0, 1).reshape((N_FSDP * SEQS * 2 * SPAN,) + field.shape[2:])

def attend(operands):
    query, keys, values, places = operands
    length = places.shape[0]
    grouped = query.reshape(length, KV_HEADS, HEADS // KV_HEADS, HEAD_DIM)
    raw_scores = low_back(jnp.einsum('qghd,kgd->ghqk', grouped, keys, precision=lax.Precision.HIGHEST)) * HEAD_DIM ** (-0.5)
    allowed = places[None, None, :, None] >= places[None, None, None, :]
    scores = jnp.where(allowed, raw_scores, -1e+30)
    row_max = lax.optimization_barrier(jnp.max(scores, axis=-1, keepdims=True))
    powers = jnp.exp(scores - row_max)
    probs = low(powers / lax.optimization_barrier(jnp.sum(powers, axis=-1, keepdims=True)))
    mixed = jnp.einsum('ghqk,kgd->qghd', probs, values, precision=lax.Precision.HIGHEST)
    return mixed.reshape(length, HEADS * HEAD_DIM)

def group_layer(rows_in, table_rows, weights):
    w_query, w_key, w_value, w_out, w_gate, w_up, w_down, gain_attn, gain_ffn = weights
    places = group_places(table_rows)
    cosine, sine_part = rope_tables(places)
    normed_one = low(rms_norm(rows_in, gain_attn))
    query = low(rotate(low_back(matmul(normed_one, w_query)).reshape(-1, HEADS, HEAD_DIM), cosine, sine_part))
    keys = low(rotate(low_back(matmul(normed_one, w_key)).reshape(-1, KV_HEADS, HEAD_DIM), cosine, sine_part))
    values = low(low_back(matmul(normed_one, w_value))).reshape(-1, KV_HEADS, HEAD_DIM)
    mixed = lax.map(jax.checkpoint(attend), (by_sequence(query), by_sequence(keys), by_sequence(values), by_sequence(places)))
    attended = low(low_back(from_sequence(mixed)))
    hidden = rows_in + low_back(matmul(attended, w_out))
    normed_two = low(rms_norm(hidden, gain_ffn))
    gate = low_back(matmul(normed_two, w_gate))
    upward = low_back(matmul(normed_two, w_up))
    inner = low(jax.nn.silu(gate) * upward)
    return hidden + low_back(matmul(inner, w_down))

def reference(tokens, span_table, w_query, w_key, w_value, w_out, w_gate, w_up, w_down, gain_attn, gain_ffn, cotangent):
    weights = tuple((item.astype(jnp.float32) for item in (w_query, w_key, w_value, w_out, w_gate, w_up, w_down, gain_attn, gain_ffn)))
    group_rows = N_FSDP * TOK_DEV
    rows_all = tokens.astype(jnp.float32).reshape(N_FSDP, N_DP, TOK_DEV, D).transpose(1, 0, 2, 3).reshape(N_DP, group_rows, D)
    grads_all = cotangent.astype(jnp.float32).reshape(N_FSDP, N_DP, TOK_DEV, D).transpose(1, 0, 2, 3).reshape(N_DP, group_rows, D)
    tables = span_table.reshape(N_DP, SEQS, 2 * N_FSDP)

    def step(totals, operands):
        rows_in, table_rows, grad_rows = operands
        result, pullback = jax.vjp(lambda inputs, params: group_layer(inputs, table_rows, params), rows_in, weights)
        grad_inputs, grad_params = pullback(grad_rows)
        totals = jax.tree.map(lambda first, second: first + second, totals, grad_params)
        return (totals, (result.astype(jnp.bfloat16), grad_inputs))
    zeros = tuple((jnp.zeros_like(item) for item in weights))
    totals, (outputs, grad_inputs) = lax.scan(step, zeros, (rows_all, tables, grads_all))

    def restore(field):
        return field.reshape(N_DP, N_FSDP, TOK_DEV, D).transpose(1, 0, 2, 3).reshape(TOKENS, D)
    return (restore(outputs), restore(grad_inputs), totals[0], totals[1], totals[2], totals[3], totals[4], totals[5], totals[6], totals[7], totals[8])
```

```python
import functools
import jax
import jax.numpy as jnp
from jax import lax
from jax.experimental import pallas as pl
from jax.experimental.pallas import tpu as pltpu
from jax.sharding import PartitionSpec as P

HEADS = 15
KV_HEADS = 5
HEAD_DIM = 64
NEG = -1e30


def product(left, right, contract):
    return lax.dot_general(
        left, right, (contract, ((), ())), preferred_element_type=jnp.float32
    )


ROW_ROW = ((1,), (1,))
PLAIN = ((1,), (0,))


def attend_kernel(tile, query_ref, key_ref, value_t_ref, qplace_ref, kplace_ref, out_ref, lse_ref):
    keys = key_ref[0, 0]
    values_t = value_t_ref[0, 0]
    kplace = kplace_ref[0]

    @pl.loop(0, query_ref.shape[2] // tile)
    def _(step):
        rows = pl.ds(pl.multiple_of(step * tile, tile), tile)
        query = query_ref[0, 0, rows]
        scores = product(keys, query, ROW_ROW)
        allowed = kplace <= qplace_ref[0, step]
        scores = jnp.where(allowed, scores, NEG)
        top = jnp.max(scores, axis=0, keepdims=True)
        powers = jnp.exp(scores - top)
        total = jnp.sum(powers, axis=0, keepdims=True)
        mixed = product(values_t, powers.astype(jnp.bfloat16), PLAIN) / total
        out_ref[0, 0, rows] = mixed.T.astype(jnp.bfloat16)
        lse_ref[0, 0, step] = top + jnp.log(total)


def attend_back_kernel(
    tile,
    query_ref,
    key_ref,
    key_t_ref,
    value_ref,
    grad_ref,
    lse_ref,
    qplace_ref,
    kplace_ref,
    dq_ref,
    dk_ref,
    dv_ref,
):
    keys = key_ref[0, 0]
    keys_t = key_t_ref[0, 0]
    values = value_ref[0, 0]
    kplace = kplace_ref[0]
    dk_ref[...] = jnp.zeros_like(dk_ref)
    dv_ref[...] = jnp.zeros_like(dv_ref)

    @pl.loop(0, query_ref.shape[2] // tile)
    def _(step):
        rows = pl.ds(pl.multiple_of(step * tile, tile), tile)
        query = query_ref[0, 0, rows]
        grad = grad_ref[0, 0, rows]
        scores = product(keys, query, ROW_ROW)
        allowed = kplace <= qplace_ref[0, step]
        probs = jnp.exp(jnp.where(allowed, scores, NEG) - lse_ref[0, 0, step])
        dv_ref[0, 0] += product(probs.astype(jnp.bfloat16), grad, PLAIN)
        dprobs = product(values, grad, ROW_ROW)
        centre = jnp.sum(probs * dprobs, axis=0, keepdims=True)
        dscores = (probs * (dprobs - centre)).astype(jnp.bfloat16)
        dk_ref[0, 0] += product(dscores, query, PLAIN)
        dq_ref[0, 0, rows] = product(keys_t, dscores, PLAIN).T * HEAD_DIM**-0.5


def block(shape):
    return pl.BlockSpec((1, 1) + shape, lambda h, s: (h, s) + (0,) * len(shape))


def by_seq(shape):
    return pl.BlockSpec((1,) + shape, lambda h, s: (s,) + (0,) * len(shape))


def attend(query, keys, values_t, qplace, kplace):
    heads, seqs, rows, dim = query.shape
    length = keys.shape[2]
    tiles, tile = qplace.shape[1], qplace.shape[3]
    return pl.pallas_call(
        functools.partial(attend_kernel, tile),
        grid=(heads, seqs),
        in_specs=[
            block((rows, dim)),
            block((length, dim)),
            block((dim, length)),
            by_seq((tiles, 1, tile)),
            by_seq((length, 1)),
        ],
        out_specs=[block((rows, dim)), block((tiles, 1, tile))],
        out_shape=[
            jax.ShapeDtypeStruct((heads, seqs, rows, dim), jnp.bfloat16),
            jax.ShapeDtypeStruct((heads, seqs, tiles, 1, tile), jnp.float32),
        ],
        cost_estimate=pl.CostEstimate(
            flops=16 * heads * seqs * rows * length * dim,
            bytes_accessed=4 * heads * seqs * (rows + length) * dim * 2,
            transcendentals=heads * seqs * rows * length,
        ),
        compiler_params=pltpu.CompilerParams(vmem_limit_bytes=40 * 2**20),
        name="attend",
    )(query, keys, values_t, qplace, kplace)


def attend_back(query, keys, keys_t, values, grad, lse, qplace, kplace):
    heads, seqs, rows, dim = query.shape
    length = keys.shape[2]
    tiles, tile = qplace.shape[1], qplace.shape[3]
    return pl.pallas_call(
        functools.partial(attend_back_kernel, tile),
        grid=(heads, seqs),
        in_specs=[
            block((rows, dim)),
            block((length, dim)),
            block((dim, length)),
            block((length, dim)),
            block((rows, dim)),
            block((tiles, 1, tile)),
            by_seq((tiles, 1, tile)),
            by_seq((length, 1)),
        ],
        out_specs=[block((rows, dim)), block((length, dim)), block((length, dim))],
        out_shape=[
            jax.ShapeDtypeStruct((heads, seqs, rows, dim), jnp.float32),
            jax.ShapeDtypeStruct((heads, seqs, length, dim), jnp.float32),
            jax.ShapeDtypeStruct((heads, seqs, length, dim), jnp.float32),
        ],
        cost_estimate=pl.CostEstimate(
            flops=40 * heads * seqs * rows * length * dim,
            bytes_accessed=4 * heads * seqs * (rows + length) * dim * 4,
            transcendentals=heads * seqs * rows * length,
        ),
        compiler_params=pltpu.CompilerParams(vmem_limit_bytes=48 * 2**20),
        name="attend_back",
    )(query, keys, keys_t, values, grad, lse, qplace, kplace)


epsilon = 1e-05
rope_base = 100000.0
ROWS = ("fsdp", "dz", "core")


def rope_tables(places, head_dim):
    half_dim = head_dim // 2
    rates = rope_base ** (-2.0 * jnp.arange(half_dim, dtype=jnp.float32) / head_dim)
    angles = places.astype(jnp.float32)[:, None] * rates[None, :]
    return (jnp.cos(angles)[:, None, :], jnp.sin(angles)[:, None, :])


def rotate(field, cosine, sine_part):
    half_dim = field.shape[-1] // 2
    first = field[..., :half_dim]
    second = field[..., half_dim:]
    return jnp.concatenate(
        [first * cosine - second * sine_part, second * cosine + first * sine_part], axis=-1
    )


def rms_scale(values):
    return lax.rsqrt(jnp.mean(values * values, axis=-1, keepdims=True) + epsilon)


def norm_back(grad_normed, values, scale_rows, gain):
    scaled = values * scale_rows
    weighted = grad_normed * gain
    grad_values = scale_rows * (
        weighted - scaled * jnp.mean(weighted * scaled, axis=-1, keepdims=True)
    )
    return (grad_values, jnp.sum(grad_normed * scaled, axis=0))


def ein(spec, left, right):
    return jnp.einsum(spec, left, right, preferred_element_type=jnp.float32)


def gather(shard, axes):
    return lax.all_gather(shard, axes, axis=0, tiled=True)


def scatter(field, axes):
    return lax.psum_scatter(field, axes, scatter_dimension=0, tiled=True)


def both_cores(part):
    other = lax.ppermute(part, "core", [(0, 1), (1, 0)])
    first_core = lax.axis_index("core") == 0
    return (
        jnp.where(first_core, part, other).astype(jnp.float32),
        jnp.where(first_core, other, part).astype(jnp.float32),
    )


def on_device(
    tokens,
    span_table,
    w_query,
    w_key,
    w_value,
    w_out,
    w_gate,
    w_up,
    w_down,
    gain_attn,
    gain_ffn,
    cotangent,
):
    bf16 = jnp.bfloat16
    groups = lax.axis_size("fsdp")
    index = lax.axis_index("fsdp")
    core = lax.axis_index("core")
    first_core = core == 0
    rows, width = tokens.shape
    seqs = span_table.shape[0]
    span = rows // (2 * seqs)
    per_kv = HEADS // KV_HEADS
    length = groups * 2 * span
    kv_width = w_key.shape[1]
    qkv_width = width + 2 * kv_width
    half = qkv_width // 2

    projections = jnp.concatenate([w_query, w_key, w_value], axis=1)
    early = jnp.concatenate(
        [
            jnp.where(first_core, projections[:, :half], projections[:, half:]),
            jnp.where(first_core, gain_attn, gain_ffn)[:, None],
        ],
        axis=1,
    )
    early_full = gather(early, ("core", "fsdp")).reshape(2, width, half + 1)
    qkv_full = early_full[:, :, :half]
    gains = early_full[:, :, half].astype(jnp.float32)
    attn_gain, ffn_gain = gains[0], gains[1]
    half_out = width // 2
    out_full = gather(
        jnp.where(first_core, w_out[:, :half_out], w_out[:, half_out:]), ("core", "fsdp")
    ).reshape(2, width, half_out)
    ffn_full = gather(jnp.where(first_core, w_gate, w_up), ("core", "fsdp")).reshape(
        2, width, w_gate.shape[1]
    )
    half_down = w_down.shape[0] // 2
    down_full = gather(
        jnp.where(first_core, w_down[:half_down], w_down[half_down:]), ("fsdp", "core")
    )

    offsets = jnp.arange(span, dtype=jnp.int32)
    mine = lax.dynamic_slice_in_dim(span_table, 2 * index, 2, 1)
    query_place = (mine[:, :, None] * span + offsets).reshape(seqs, 2 * span)
    key_place = (span_table[:, :, None] * span + offsets).reshape(seqs, length, 1)
    tile_place = jnp.broadcast_to(
        query_place.reshape(seqs, 1, 2, 1, span), (seqs, per_kv, 2, 1, span)
    ).reshape(seqs, per_kv * 2, 1, span)
    cosine, sine_part = rope_tables(query_place.reshape(-1), HEAD_DIM)
    inputs = tokens.astype(jnp.float32)
    scale_one = rms_scale(inputs)
    normed_one = (inputs * scale_one * attn_gain).astype(bf16)
    halves = ein("rd,bde->bre", normed_one, qkv_full)
    qkv = jnp.concatenate([halves[0], halves[1]], axis=1)
    query_rows = rotate(
        qkv[:, :width].reshape(rows, HEADS, HEAD_DIM), cosine, sine_part
    ).astype(bf16) * jnp.asarray(HEAD_DIM**-0.5, bf16)
    key_rows = rotate(
        qkv[:, width : width + kv_width].reshape(rows, KV_HEADS, HEAD_DIM), cosine, sine_part
    ).astype(bf16)
    key_value = jnp.concatenate(
        [key_rows.reshape(rows, kv_width), qkv[:, width + kv_width :].astype(bf16)], axis=1
    )
    spread = gather(key_value, "fsdp").reshape(
        groups, seqs, 2 * span, 2, KV_HEADS, HEAD_DIM
    )
    key_value_heads = spread.transpose(3, 4, 1, 0, 2, 5).reshape(
        2, KV_HEADS, seqs, length, HEAD_DIM
    )
    keys, values = key_value_heads[0], key_value_heads[1]
    turned = spread.transpose(3, 4, 1, 5, 0, 2).reshape(2, KV_HEADS, seqs, HEAD_DIM, length)
    keys_t, values_t = turned[0], turned[1]

    def to_heads(field):
        return (
            field.reshape(seqs, 2 * span, KV_HEADS, per_kv, HEAD_DIM)
            .transpose(2, 0, 3, 1, 4)
            .reshape(KV_HEADS, seqs, per_kv * 2 * span, HEAD_DIM)
        )

    def from_heads(field):
        return (
            field.reshape(KV_HEADS, seqs, per_kv, 2 * span, HEAD_DIM)
            .transpose(1, 3, 0, 2, 4)
            .reshape(rows, HEADS * HEAD_DIM)
        )

    query_heads = to_heads(query_rows)
    mixed_heads, log_sums = attend(query_heads, keys, values_t, tile_place, key_place)
    attended = from_heads(mixed_heads)
    hidden = inputs + ein("rd,bde->rbe", attended, out_full).reshape(rows, width)
    scale_two = rms_scale(hidden)
    normed_two = (hidden * scale_two * ffn_gain).astype(bf16)
    both = ein("rd,bde->bre", normed_two, ffn_full)
    gate, upward = both[0], both[1]
    sigma = jax.nn.sigmoid(gate)
    activated = gate * sigma
    inner = (activated * upward).astype(bf16)
    output = (hidden + ein("re,ed->rd", inner, down_full)).astype(bf16)

    grad_out = cotangent.astype(jnp.float32)
    grad_down = ein("re,rd->ed", inner, cotangent).astype(bf16)
    grad_inner = ein("rd,ed->re", cotangent, down_full)
    grad_gate = (grad_inner * upward * sigma * (1.0 + gate * (1.0 - sigma))).astype(bf16)
    grad_up = (grad_inner * activated).astype(bf16)
    grad_both = jnp.stack([grad_gate, grad_up])
    grad_ffn = ein("rd,bre->bde", normed_two, grad_both).astype(bf16).reshape(2 * width, -1)
    grad_normed_two = ein("bre,bde->rd", grad_both, ffn_full)
    grad_hidden_norm, grad_gain_ffn = norm_back(grad_normed_two, hidden, scale_two, ffn_gain)
    grad_hidden = grad_out + grad_hidden_norm
    grad_branch = grad_hidden.astype(bf16)
    branch_halves = grad_branch.reshape(rows, 2, half_out)
    grad_proj = ein("rd,rbe->bde", attended, branch_halves).astype(bf16).reshape(2 * width, -1)
    grad_attended = ein("rbe,bde->rd", branch_halves, out_full).astype(bf16)
    grad_attended, grad_down, grad_ffn, grad_proj = lax.optimization_barrier(
        (grad_attended, grad_down, grad_ffn, grad_proj)
    )
    down_part = scatter(grad_down, ("fsdp", "core"))
    ffn_part = scatter(grad_ffn, ("core", "fsdp"))
    out_part = scatter(grad_proj, ("core", "fsdp"))
    grad_query_heads, grad_key_heads, grad_value_heads = attend_back(
        query_heads,
        keys,
        keys_t,
        values,
        to_heads(grad_attended),
        log_sums,
        tile_place,
        key_place,
    )
    grad_spread = (
        jnp.stack([grad_key_heads, grad_value_heads])
        .astype(bf16)
        .reshape(2, KV_HEADS, seqs, groups, 2 * span, HEAD_DIM)
        .transpose(3, 2, 4, 0, 1, 5)
        .reshape(groups * rows, 2 * kv_width)
    )
    grad_spread, down_part, ffn_part, out_part = lax.optimization_barrier(
        (grad_spread, down_part, ffn_part, out_part)
    )
    grad_key_value = scatter(grad_spread, "fsdp")
    grad_key_rows = rotate(
        grad_key_value[:, :kv_width].astype(jnp.float32).reshape(rows, KV_HEADS, HEAD_DIM),
        cosine,
        -sine_part,
    )
    grad_query_rows = rotate(
        from_heads(grad_query_heads).reshape(rows, HEADS, HEAD_DIM), cosine, -sine_part
    )
    grad_qkv = jnp.concatenate(
        [
            grad_query_rows.reshape(rows, width).astype(bf16),
            grad_key_rows.reshape(rows, kv_width).astype(bf16),
            grad_key_value[:, kv_width:],
        ],
        axis=1,
    )
    grad_halves = jnp.stack([grad_qkv[:, :half], grad_qkv[:, half:]])
    grad_normed_one = ein("bre,bde->rd", grad_halves, qkv_full)
    grad_input_norm, grad_gain_attn = norm_back(grad_normed_one, inputs, scale_one, attn_gain)
    grad_tokens = grad_hidden + grad_input_norm
    grad_gains = jnp.stack([grad_gain_attn, grad_gain_ffn])[:, :, None]
    grad_early = (
        jnp.concatenate([ein("rd,bre->bde", normed_one, grad_halves), grad_gains], axis=2)
        .astype(bf16)
        .reshape(2 * width, half + 1)
    )
    sums = lax.psum((down_part, ffn_part, out_part), "dz")
    grad_early, down_sum, ffn_sum, out_sum = lax.optimization_barrier((grad_early,) + tuple(sums))
    early_part = scatter(grad_early, ("core", "fsdp"))
    early_sum = lax.psum(early_part, "dz")

    down_both = jnp.concatenate(both_cores(down_sum), axis=0)
    ffn_both = both_cores(ffn_sum)
    out_both = both_cores(out_sum)
    early_both = both_cores(early_sum)
    grad_projections = jnp.concatenate([early_both[0][:, :half], early_both[1][:, :half]], axis=1)
    return (
        output,
        grad_tokens,
        grad_projections[:, :width],
        grad_projections[:, width : width + kv_width],
        grad_projections[:, width + kv_width :],
        jnp.concatenate([out_both[0], out_both[1]], axis=1),
        ffn_both[0],
        ffn_both[1],
        down_both,
        early_both[0][:, half],
        early_both[1][:, half],
    )


def solution(mesh):
    fsdp = mesh.shape["fsdp"]
    split = jax.sharding.Mesh(mesh.devices.reshape(fsdp, -1, 2), ROWS)
    weight = P("fsdp", None)
    row = P(ROWS, None)
    return jax.shard_map(
        on_device,
        mesh=split,
        in_specs=(row, P(("dz", "core"), None)) + (weight,) * 7 + (P("fsdp"),) * 2 + (row,),
        out_specs=(row, row) + (weight,) * 7 + (P("fsdp"),) * 2,
        check_vma=False,
    )
```
